32 devices in a mesh: group: 2 (over x), ep: 16 (over z, y, core).
Axes of the slice: x: 2, y: 2, z: 4, core: 2. Of those that a mesh axis runs over, the one named last changes fastest.
Arguments:
- query: bfloat16 [128, 4096], P(('group', 'ep')), parts along dimension 0, may hold values from -6 to 6
- fresh_key: bfloat16 [128, 256], P(('group', 'ep')), parts along dimension 0, may hold values from -6 to 6
- fresh_value: bfloat16 [128, 256], P(('group', 'ep')), parts along dimension 0, may hold values from -6 to 6
- stored_keys: bfloat16 [128, 512, 256], P(('group', 'ep')), parts along dimension 0, may hold values from -30 to 30
- stored_values: bfloat16 [128, 512, 256], P(('group', 'ep')), parts along dimension 0, may hold values from -6 to 6
- lengths: int32 [128], P(('group', 'ep')), parts along dimension 0, may hold values from 2 to 512, as said below
- q_gain: float32 [128], replicated, may hold values from 0.1 to 1.9
- key_norm_gain: float32 [128], replicated, may hold values from 0.1 to 1.9
- expert_input: bfloat16 [2048, 2048], P(('group', 'ep')), parts along dimension 0, may hold values from -6 to 6
- routing: int32 [2048, 8], P(('group', 'ep')), parts along dimension 0, may hold values from 0 to 15, all different within a row; in each aligned block of 64 rows (0 to 63, 64 to 127, ...) at most 64 rows name the same one
- gate_weights: float32 [2048, 8], P(('group', 'ep')), parts along dimension 0, may hold values from 0.05 to 1
- w_gate_up: bfloat16 [16, 2048, 1536], P('ep'), may hold values from -0.125 to 0.125
- w_down: bfloat16 [16, 768, 2048], P('ep'), may hold values from -0.21875 to 0.21875
Outputs:
- attention_out: bfloat16 [128, 4096], P(('group', 'ep')), parts along dimension 0
- expert_out: bfloat16 [2048, 2048], P(('group', 'ep')), parts along dimension 0
The draws below stay inside these ranges and needn't reach their ends.
There are 2 independent parts, one for each index of `group`. The reference program is written for one: setup_inputs(seed, part) draws one part's arguments, and reference() takes and returns one part's arrays. A program takes and returns all parts, laid end to end along the dimension named above; an argument that names none is the same for every part. Nothing has to cross between parts.
Inputs may be any that keep to these rules, and one draw needn't show every extreme that they name: `routing`: each row names 8 different experts; among the rows of one device no expert is named more than 64 times, a bound that some block reaches. The new token stands at position lengths; some row has 512.
All inputs are finite; a program needn't handle non-finite values.
Results may differ from the reference program's by a relative error of at most 0.0063.
Values may be sent and summed in bfloat16 or wider, within the bound.
A program may use at most 64 MiB of HBM per device.

```python
import math
import jax
import jax.numpy as jnp
import numpy as np
from jax import lax

D = 2048
HID = 768
TOPK = 8
QUERY_HEADS = 32
KEY_VALUE_HEADS = 2
HEAD_SIZE = 128
R_DEV = 64
CACHE_SPAN = 512
EXPERTS = 16
TOKENS = 1024
ATTENTION_ROWS = 64
CAP = 64
N_EP = 16


def query_values(key):
    base = jax.random.fold_in(key, 101)
    normal_part = jnp.clip(jax.random.normal(jax.random.fold_in(base, 1), (ATTENTION_ROWS, QUERY_HEADS * HEAD_SIZE), jnp.float32), -6.0, 6.0)
    return normal_part


def row_lengths(key):
    base = jax.random.fold_in(key, 202)
    drawn = jax.random.randint(jax.random.fold_in(base, 1), (ATTENTION_ROWS,), 2, CACHE_SPAN + 1)
    chosen = jax.random.randint(jax.random.fold_in(base, 2), (), 0, ATTENTION_ROWS)
    return drawn.at[chosen].set(CACHE_SPAN).astype(jnp.int32)


def draw_query(key, part):
    all_values = query_values(key)
    return all_values.astype(jnp.bfloat16)


def draw_lengths(key, part):
    return row_lengths(key)


def draw_stored_keys(key, part):
    key = jax.random.fold_in(key, 3)
    drawn_scores = jnp.clip(jax.random.normal(key, (ATTENTION_ROWS, CACHE_SPAN, KEY_VALUE_HEADS, HEAD_SIZE), jnp.float32), -6.0, 6.0)
    return drawn_scores.reshape(ATTENTION_ROWS, CACHE_SPAN, KEY_VALUE_HEADS * HEAD_SIZE).astype(jnp.bfloat16)


def shard_levels(stream_key, extent, cuts, least, top_value):
    level = 1.0
    for position, shards_of in cuts:
        heights = jax.random.uniform(jax.random.fold_in(jax.random.fold_in(stream_key, 6), position), (shards_of,), jnp.float32, least / len(cuts), top_value / len(cuts))
        level = level * jnp.repeat(jnp.exp(heights), extent[position] // shards_of).reshape((-1,) + (1,) * (len(extent) - 1 - position))
    return level


def deal_out(stream_key, own, number, rows, amount, top, most, lean):
    order = jax.random.permutation(stream_key, amount)
    crowded, usual = portions_of(amount, rows * top, most, lean, True), portions_of(amount, rows * top, most, lean, False)
    places = jnp.arange(amount)

    def named(sizes, turn):
        used = int((sizes > 0).sum())
        fixed = max(1, used // 4)
        moved = fixed + (places - fixed + turn * (used - fixed)) % max(1, amount - fixed)
        return jnp.zeros((amount,), jnp.int32).at[order[jnp.where(places < fixed, places, moved)]].set(jnp.asarray(sizes, jnp.int32))

    sizes = jnp.where(number % 4 == 0, named(crowded, number // 4), named(usual, number - number // 4 - 1))
    mixed = jax.random.permutation(jax.random.fold_in(own, 3), amount)
    giver, sink = mixed[0:amount // 2 * 2:2], mixed[1:amount // 2 * 2:2]
    room = jnp.minimum(sizes[giver] - 1, most - sizes[sink]) // 2
    room = jnp.where((giver == order[0]) | (sink == order[0]) | (sizes[sink] == 0), 0, jnp.maximum(room, 0))
    moved = jax.random.randint(jax.random.fold_in(own, 4), (amount // 2,), 0, 1 << 20) % (room + 1)
    sizes = sizes.at[giver].add(-moved).at[sink].add(moved)
    members = jnp.searchsorted(jnp.cumsum(sizes), jnp.arange(rows * top), side="right").astype(jnp.int32)
    listing = members.reshape(top, rows).T
    listing = listing[jax.random.permutation(jax.random.fold_in(own, 1), rows)]
    turn = jax.random.randint(jax.random.fold_in(own, 2), (rows, 1), 0, top)
    return jnp.take_along_axis(listing, (jnp.arange(top)[None, :] + turn) % top, axis=1)


def portions_of(amount, total, limit, skew, full):
    loads = [(1 << 20) // math.isqrt(grade ** skew) + 1 for grade in range(1, amount + 1)]
    largest = limit if full else min(limit, max(-(-total // amount), total * loads[0] // sum(loads)))
    least = 1 if total - largest >= amount - 1 else 0
    counts, spare = [largest] + [least] * (amount - 1), total - largest - least * (amount - 1)
    while spare > 0:
        candidates = [i for i in range(1, amount) if counts[i] < largest] or [i for i in range(1, amount) if counts[i] < limit]
        mass, remaining = sum([loads[i] for i in candidates]), spare
        for i in candidates:
            extra = min(limit - counts[i], max(1, remaining * loads[i] // mass), spare)
            counts[i] = counts[i] + extra
            spare = spare - extra
    return np.array(counts)


def normal_values(stream_key, extent, width, bound, split=(), kind=jnp.bfloat16):
    array = jax.random.normal(stream_key, extent, jnp.float32) * width
    if len(split) > 0:
        array = shard_levels(stream_key, extent, split, -0.22, 0.18) * array
    return jnp.clip(array, min=-bound, max=bound).astype(kind)


def setup_inputs(seed: int = 0, part: int = 0) -> dict:
    key_of = jax.random.split(jax.random.key(seed), 14)
    part_splits = jax.random.split(jax.random.fold_in(key_of[13], part), 14)
    query = draw_query(jax.random.fold_in(jax.random.fold_in(key_of[13], part), 71), part)
    fresh_key = normal_values(part_splits[1], (ATTENTION_ROWS, KEY_VALUE_HEADS * HEAD_SIZE), 1.0, 6.0, ((0, 16),))
    fresh_value = normal_values(part_splits[2], (ATTENTION_ROWS, KEY_VALUE_HEADS * HEAD_SIZE), 1.0, 6.0, ((0, 16),))
    stored_keys = draw_stored_keys(jax.random.fold_in(jax.random.fold_in(key_of[13], part), 71), part)
    stored_values = normal_values(part_splits[4], (ATTENTION_ROWS, CACHE_SPAN, KEY_VALUE_HEADS * HEAD_SIZE), 1.0, 6.0, ((0, 16),))
    lengths = draw_lengths(jax.random.fold_in(jax.random.fold_in(key_of[13], part), 71), part)
    q_gain = jnp.clip(1.0 + 0.18 * jax.random.normal(key_of[6], (HEAD_SIZE,), jnp.float32), 0.1, 1.9)
    key_norm_gain = jnp.clip(1.0 + 0.18 * jax.random.normal(key_of[7], (HEAD_SIZE,), jnp.float32), 0.1, 1.9)
    expert_input = normal_values(part_splits[8], (TOKENS, D), 1.0, 6.0, ((0, 16),))
    routing_keys = jax.random.split(jax.random.fold_in(part_splits[9], 1), TOKENS // R_DEV)
    routing_turns = jax.random.permutation(jax.random.fold_in(part_splits[9], 3), TOKENS // R_DEV)
    routing = jax.vmap(lambda own, number: deal_out(jax.random.fold_in(part_splits[9], 2), own, number, R_DEV, EXPERTS, TOPK, CAP, 2))(routing_keys, routing_turns).reshape((TOKENS, TOPK))
    gate_weights = jnp.clip(jnp.exp(math.log(1.0) - 2.9957323 * jax.random.uniform(part_splits[10], (TOKENS, TOPK), jnp.float32) ** shard_levels(part_splits[10], (TOKENS, TOPK), ((0, 16),), -0.2, 0.2)), 0.05, 1.0)
    w_gate_up = normal_values(key_of[11], (EXPERTS, D, 2 * HID), D ** -0.5, 0.125, ((0, 16),))
    w_down = normal_values(key_of[12], (EXPERTS, HID, D), HID ** -0.5, 0.21875, ((0, 16),))
    return {"query": query, "fresh_key": fresh_key, "fresh_value": fresh_value, "stored_keys": stored_keys, "stored_values": stored_values, "lengths": lengths, "q_gain": q_gain, "key_norm_gain": key_norm_gain, "expert_input": expert_input, "routing": routing, "gate_weights": gate_weights, "w_gate_up": w_gate_up, "w_down": w_down}


def apply_rotation(all_values, positions):
    half = all_values.shape[-1] // 2
    steps = jnp.arange(half).astype(jnp.float32)
    inverse = jnp.exp(-2.0 * steps / all_values.shape[-1] * jnp.log(jnp.float32(1000000.0)))
    angles = positions.astype(jnp.float32)[:, None] * inverse[None, :]
    cosine = jnp.cos(angles)[:, None, :]
    sine = jnp.sin(angles)[:, None, :]
    first = all_values[..., :half]
    second = all_values[..., half:]
    return jnp.concatenate([first * cosine - second * sine, second * cosine + first * sine], axis=-1)

def per_head_norm(all_values, gain):
    scale = lax.rsqrt(lax.optimization_barrier(jnp.mean(all_values * all_values, axis=-1, keepdims=True)) + 1e-06)
    return all_values * scale * gain

def attention(query, fresh_key, fresh_value, stored_keys, stored_values, lengths, q_gain, key_norm_gain):
    token_count = query.shape[0]
    query_groups = QUERY_HEADS // KEY_VALUE_HEADS
    normalized_query = apply_rotation(per_head_norm(query.astype(jnp.float32).reshape(token_count, QUERY_HEADS, HEAD_SIZE), q_gain), lengths).astype(jnp.bfloat16)
    normalized_key = apply_rotation(per_head_norm(fresh_key.astype(jnp.float32).reshape(token_count, KEY_VALUE_HEADS, HEAD_SIZE), key_norm_gain), lengths).astype(jnp.bfloat16)
    grouped_queries = normalized_query.reshape(token_count, KEY_VALUE_HEADS, query_groups, HEAD_SIZE).astype(jnp.float32)
    all_keys = stored_keys.reshape(token_count, CACHE_SPAN, KEY_VALUE_HEADS, HEAD_SIZE).astype(jnp.float32)
    scores = jnp.einsum('rhgd,rchd->rhgc', grouped_queries, all_keys) / jnp.sqrt(jnp.float32(HEAD_SIZE))
    own = jnp.einsum('rhgd,rhd->rhg', grouped_queries, normalized_key.astype(jnp.float32)) / jnp.sqrt(jnp.float32(HEAD_SIZE))
    live = jnp.arange(CACHE_SPAN).astype(jnp.int32)[None, :] < lengths[:, None]
    scores = jnp.where(live[:, None, None, :], scores, -jnp.inf)
    top = jnp.maximum(lax.optimization_barrier(jnp.max(scores, axis=-1)), own)
    weights = jnp.exp(scores - top[..., None])
    own_weight = jnp.exp(own - top)
    total = lax.optimization_barrier(jnp.sum(weights, axis=-1)) + own_weight
    probs = (weights / total[..., None]).astype(jnp.bfloat16)
    fresh_token_prob = (own_weight / total).astype(jnp.bfloat16)
    all_values = stored_values.reshape(token_count, CACHE_SPAN, KEY_VALUE_HEADS, HEAD_SIZE).astype(jnp.float32)
    mixed_output = jnp.einsum('rhgc,rchd->rhgd', probs.astype(jnp.float32), all_values)
    mixed_output = mixed_output + fresh_token_prob.astype(jnp.float32)[..., None] * fresh_value.astype(jnp.float32).reshape(token_count, KEY_VALUE_HEADS, 1, HEAD_SIZE)
    return mixed_output.reshape(token_count, QUERY_HEADS * HEAD_SIZE).astype(jnp.bfloat16)

def expert_layer(expert_input, routing, gate_weights, w_gate_up, w_down):
    token_count = expert_input.shape[0]
    share = gate_weights / lax.optimization_barrier(jnp.sum(gate_weights, axis=1, keepdims=True))
    padded = jnp.concatenate([expert_input, jnp.zeros((1, D), jnp.bfloat16)], axis=0)
    owner = (jnp.arange(token_count) // R_DEV).astype(jnp.int32)
    row_ids = jnp.arange(token_count).astype(jnp.int32)

    def one_expert(total, expert):
        hits = routing == expert
        hit = jnp.any(hits, axis=1)
        blocks = hit.reshape(N_EP, R_DEV).astype(jnp.int32)
        place = (jnp.cumsum(blocks, axis=1) - blocks).reshape(-1)
        slot = jnp.where(hit, owner * CAP + place, N_EP * CAP).astype(jnp.int32)
        table = jnp.full((N_EP * CAP + 1,), token_count, jnp.int32).at[slot].set(row_ids)
        rows = padded[table[:-1]]
        both = jnp.dot(rows, w_gate_up[expert], preferred_element_type=jnp.float32)
        hidden = (jax.nn.silu(both[:, :HID]) * both[:, HID:]).astype(jnp.bfloat16)
        answer = jnp.dot(hidden, w_down[expert], preferred_element_type=jnp.float32).astype(jnp.bfloat16)
        answer = jnp.concatenate([answer, jnp.zeros((1, D), jnp.bfloat16)], axis=0)
        picked = answer[slot].astype(jnp.float32)
        weight = lax.optimization_barrier(jnp.sum(jnp.where(hits, share, jnp.float32(0.0)), axis=1))
        return (total + weight[:, None] * picked, None)
    total, _ = lax.scan(one_expert, jnp.zeros((token_count, D), jnp.float32), jnp.arange(EXPERTS).astype(jnp.int32))
    return total.astype(jnp.bfloat16)

def reference(query, fresh_key, fresh_value, stored_keys, stored_values, lengths, q_gain, key_norm_gain, expert_input, routing, gate_weights, w_gate_up, w_down):
    attention_out = attention(query, fresh_key, fresh_value, stored_keys, stored_values, lengths, q_gain, key_norm_gain)
    expert_out = expert_layer(expert_input, routing, gate_weights, w_gate_up, w_down)
    return (attention_out, expert_out)
```

```python
import jax
import jax.numpy as jnp
from jax import lax
from jax.sharding import PartitionSpec as P

QUERY_HEADS = 32
KEY_VALUE_HEADS = 2
HEAD_SIZE = 128


def apply_rotation(all_values, positions):
    half = all_values.shape[-1] // 2
    steps = jnp.arange(half).astype(jnp.float32)
    inverse = jnp.exp(-2.0 * steps / all_values.shape[-1] * jnp.log(jnp.float32(1000000.0)))
    angles = positions.astype(jnp.float32)[:, None] * inverse[None, :]
    cosine = jnp.cos(angles)[:, None, :]
    sine = jnp.sin(angles)[:, None, :]
    first = all_values[..., :half]
    second = all_values[..., half:]
    return jnp.concatenate(
        [first * cosine - second * sine, second * cosine + first * sine], axis=-1
    )


def per_head_norm(all_values, gain):
    scale = lax.rsqrt(jnp.mean(all_values * all_values, axis=-1, keepdims=True) + 1e-06)
    return all_values * scale * gain


def attention(
    query, fresh_key, fresh_value, stored_keys, stored_values, lengths, q_gain, key_norm_gain
):
    token_count = query.shape[0]
    context_output = stored_keys.shape[1]
    query_groups = QUERY_HEADS // KEY_VALUE_HEADS
    normalized_query = apply_rotation(
        per_head_norm(
            query.astype(jnp.float32).reshape(token_count, QUERY_HEADS, HEAD_SIZE), q_gain
        ),
        lengths,
    ).astype(jnp.bfloat16)
    normalized_key = apply_rotation(
        per_head_norm(
            fresh_key.astype(jnp.float32).reshape(token_count, KEY_VALUE_HEADS, HEAD_SIZE),
            key_norm_gain,
        ),
        lengths,
    ).astype(jnp.bfloat16)
    grouped_queries = normalized_query.reshape(
        token_count, KEY_VALUE_HEADS, query_groups, HEAD_SIZE
    )
    all_keys = stored_keys.reshape(token_count, context_output, KEY_VALUE_HEADS, HEAD_SIZE)
    scores = jnp.einsum(
        "rhgd,rchd->rhgc", grouped_queries, all_keys, preferred_element_type=jnp.float32
    ) / jnp.sqrt(jnp.float32(HEAD_SIZE))
    own = jnp.sum(
        grouped_queries.astype(jnp.float32) * normalized_key.astype(jnp.float32)[:, :, None, :],
        axis=-1,
    ) / jnp.sqrt(jnp.float32(HEAD_SIZE))
    live = jnp.arange(context_output)[None, :] < lengths[:, None]
    scores = jnp.where(live[:, None, None, :], scores, -jnp.inf)
    top = jnp.maximum(jnp.max(scores, axis=-1), own)
    weights = jnp.exp(scores - top[..., None])
    own_weight = jnp.exp(own - top)
    total = jnp.sum(weights, axis=-1) + own_weight
    probs = (weights / total[..., None]).astype(jnp.bfloat16)
    fresh_token_prob = (own_weight / total).astype(jnp.bfloat16)
    all_values = stored_values.reshape(token_count, context_output, KEY_VALUE_HEADS, HEAD_SIZE)
    mixed_output = jnp.einsum(
        "rhgc,rchd->rhgd", probs, all_values, preferred_element_type=jnp.float32
    )
    mixed_output = mixed_output + fresh_token_prob.astype(jnp.float32)[
        ..., None
    ] * fresh_value.astype(jnp.float32).reshape(token_count, KEY_VALUE_HEADS, 1, HEAD_SIZE)
    return mixed_output.reshape(token_count, QUERY_HEADS * HEAD_SIZE).astype(jnp.bfloat16)


def feed_forward(slots, w_gate_up, w_down):
    layout = slots.shape
    flat = slots.reshape(-1, layout[-1])
    hidden_units = w_down.shape[1]
    both = jnp.dot(flat, w_gate_up[0], preferred_element_type=jnp.float32)
    hidden = (jax.nn.silu(both[:, :hidden_units]) * both[:, hidden_units:]).astype(jnp.bfloat16)
    answer = jnp.dot(hidden, w_down[0], preferred_element_type=jnp.float32).astype(jnp.bfloat16)
    return answer.reshape(layout)


def dense_experts(expert_input, routing, share, w_gate_up, w_down):
    experts_all = lax.axis_size("ep")
    hits = routing[:, :, None] == jnp.arange(experts_all)[None, None, :]
    spread = jnp.sum(jnp.where(hits, share[:, :, None], 0.0), axis=1)
    arrived = lax.all_gather(expert_input, "ep", axis=0, tiled=True)
    weight = lax.all_to_all(spread, "ep", split_axis=1, concat_axis=0, tiled=True)
    answer = feed_forward(arrived, w_gate_up, w_down).astype(jnp.float32)
    part = (weight * answer).astype(jnp.bfloat16)
    return lax.psum_scatter(part, "ep", scatter_dimension=0, tiled=True)


def local(
    query,
    fresh_key,
    fresh_value,
    stored_keys,
    stored_values,
    lengths,
    q_gain,
    key_norm_gain,
    expert_input,
    routing,
    gate_weights,
    w_gate_up,
    w_down,
):
    attention_out = attention(
        query, fresh_key, fresh_value, stored_keys, stored_values, lengths, q_gain, key_norm_gain
    )
    devices = lax.axis_size("ep")
    experts_all = devices * w_gate_up.shape[0]
    rows, width = expert_input.shape
    picks = routing.shape[1]
    share = gate_weights / jnp.sum(gate_weights, axis=1, keepdims=True)
    if devices <= 2 * picks:
        return (attention_out, dense_experts(expert_input, routing, share, w_gate_up, w_down))
    capacity = 2 * rows * picks // experts_all
    flat_ids = routing.reshape(-1)
    onehot = (flat_ids[:, None] == jnp.arange(experts_all)[None, :]).astype(jnp.int32)
    earlier = jnp.sum((jnp.cumsum(onehot, axis=0) - onehot) * onehot, axis=1)
    slot = flat_ids * capacity + earlier
    padded = jnp.concatenate([expert_input, jnp.zeros((1, width), jnp.bfloat16)], axis=0)
    sources = jnp.arange(rows * picks) // picks
    table = jnp.full((experts_all * capacity,), rows, jnp.int32).at[slot].set(sources)
    outgoing = padded[table].reshape(experts_all, capacity, width)
    arrived = lax.all_to_all(outgoing, "ep", split_axis=0, concat_axis=0, tiled=True)
    results = feed_forward(arrived, w_gate_up, w_down)
    returned = lax.all_to_all(results, "ep", split_axis=0, concat_axis=0, tiled=True)
    picked = returned.reshape(experts_all * capacity, width)[slot].reshape(rows, picks, width)
    mixed_output = jnp.zeros((rows, width), jnp.float32)
    for column in range(picks):
        mixed_output = mixed_output + share[:, column : column + 1] * picked[:, column].astype(
            jnp.float32
        )
    return (attention_out, mixed_output.astype(jnp.bfloat16))


def solution(mesh):
    return jax.shard_map(
        local,
        mesh=mesh,
        in_specs=(
            P(("group", "ep"), None),
            P(("group", "ep"), None),
            P(("group", "ep"), None),
            P(("group", "ep"), None, None),
            P(("group", "ep"), None, None),
            P(("group", "ep")),
            P(),
            P(),
            P(("group", "ep"), None),
            P(("group", "ep"), None),
            P(("group", "ep"), None),
            P("ep", None, None),
            P("ep", None, None),
        ),
        out_specs=(P(("group", "ep"), None), P(("group", "ep"), None)),
        check_vma=False,
    )
```

```python
import jax
import jax.numpy as jnp
from jax import lax
from jax.experimental import pallas as pl
from jax.experimental.pallas import tpu as pltpu
from jax.sharding import PartitionSpec as P

QUERY_HEADS = 32
KEY_VALUE_HEADS = 2
HEAD_SIZE = 128


def apply_rotation(all_values, positions):
    half = all_values.shape[-1] // 2
    steps = jnp.arange(half).astype(jnp.float32)
    inverse = jnp.exp(-2.0 * steps / all_values.shape[-1] * jnp.log(jnp.float32(1000000.0)))
    angles = positions.astype(jnp.float32)[:, None] * inverse[None, :]
    cosine = jnp.cos(angles)[:, None, :]
    sine = jnp.sin(angles)[:, None, :]
    first = all_values[..., :half]
    second = all_values[..., half:]
    return jnp.concatenate(
        [first * cosine - second * sine, second * cosine + first * sine], axis=-1
    )


def per_head_norm(all_values, gain):
    scale = lax.rsqrt(jnp.mean(all_values * all_values, axis=-1, keepdims=True) + 1e-06)
    return all_values * scale * gain


def attention(
    query, fresh_key, fresh_value, stored_keys, stored_values, lengths, q_gain, key_norm_gain
):
    token_count = query.shape[0]
    context_output = stored_keys.shape[1]
    query_groups = QUERY_HEADS // KEY_VALUE_HEADS
    normalized_query = apply_rotation(
        per_head_norm(
            query.astype(jnp.float32).reshape(token_count, QUERY_HEADS, HEAD_SIZE), q_gain
        ),
        lengths,
    ).astype(jnp.bfloat16)
    normalized_key = apply_rotation(
        per_head_norm(
            fresh_key.astype(jnp.float32).reshape(token_count, KEY_VALUE_HEADS, HEAD_SIZE),
            key_norm_gain,
        ),
        lengths,
    ).astype(jnp.bfloat16)
    grouped_queries = normalized_query.reshape(
        token_count, KEY_VALUE_HEADS, query_groups, HEAD_SIZE
    )
    all_keys = stored_keys.reshape(token_count, context_output, KEY_VALUE_HEADS, HEAD_SIZE)
    scores = jnp.einsum(
        "rhgd,rchd->rhgc", grouped_queries, all_keys, preferred_element_type=jnp.float32
    ) / jnp.sqrt(jnp.float32(HEAD_SIZE))
    own = jnp.sum(
        grouped_queries.astype(jnp.float32) * normalized_key.astype(jnp.float32)[:, :, None, :],
        axis=-1,
    ) / jnp.sqrt(jnp.float32(HEAD_SIZE))
    live = jnp.arange(context_output)[None, :] < lengths[:, None]
    scores = jnp.where(live[:, None, None, :], scores, -jnp.inf)
    top = jnp.maximum(jnp.max(scores, axis=-1), own)
    weights = jnp.exp(scores - top[..., None])
    own_weight = jnp.exp(own - top)
    total = jnp.sum(weights, axis=-1) + own_weight
    probs = (weights / total[..., None]).astype(jnp.bfloat16)
    fresh_token_prob = (own_weight / total).astype(jnp.bfloat16)
    all_values = stored_values.reshape(token_count, context_output, KEY_VALUE_HEADS, HEAD_SIZE)
    mixed_output = jnp.einsum(
        "rhgc,rchd->rhgd", probs, all_values, preferred_element_type=jnp.float32
    )
    mixed_output = mixed_output + fresh_token_prob.astype(jnp.float32)[
        ..., None
    ] * fresh_value.astype(jnp.float32).reshape(token_count, KEY_VALUE_HEADS, 1, HEAD_SIZE)
    return mixed_output.reshape(token_count, QUERY_HEADS * HEAD_SIZE).astype(jnp.bfloat16)


def feed_forward(slots, w_gate_up, w_down):
    layout = slots.shape
    flat = slots.reshape(-1, layout[-1])
    hidden_units = w_down.shape[1]
    both = jnp.dot(flat, w_gate_up[0], preferred_element_type=jnp.float32)
    hidden = (jax.nn.silu(both[:, :hidden_units]) * both[:, hidden_units:]).astype(jnp.bfloat16)
    answer = jnp.dot(hidden, w_down[0], preferred_element_type=jnp.float32).astype(jnp.bfloat16)
    return answer.reshape(layout)


LAYERS = 4
EXTRA = 128
Y_FIRST = 768
PIECE = 512
UP, DOWN, ACROSS, MATE = 0, 1, 2, 3


def expert_kernel(
    x_ref, routing_ref, gates_ref, up_hbm, down_hbm, out_ref,
    rows_all, sums, from_mate, from_across, from_layer, w_up, w_down, hidden,
    w_sem, ag_send, ag_recv, mate_send, mate_recv, across_send, across_recv, chain_send, chain_recv,
):
    me = lax.axis_index("ep")
    core, side, layer = lax.rem(me, 2), lax.rem(me // 2, 2), me // 4
    last = LAYERS - 1
    experts = LAYERS * 4
    count, width = x_ref.shape
    total = width + EXTRA
    hid = w_down.shape[0]
    mate, across = me + 1 - 2 * core, me + 2 - 4 * side
    has_up, has_down = layer < last, layer > 0
    edge = jnp.logical_or(layer == 0, layer == last)
    everyone = layer >= 0
    spans = (pl.ds(Y_FIRST, total - Y_FIRST), pl.ds(0, Y_FIRST))
    pending = []

    up_copy = pltpu.make_async_copy(up_hbm, w_up, w_sem.at[0])
    down_copy = pltpu.make_async_copy(down_hbm, w_down, w_sem.at[1])
    up_copy.start()
    down_copy.start()

    def block(l, s, c):
        return (l * 2 + s) * 2 + c

    def rows(b):
        return pl.ds(pl.multiple_of(b * count, count), count)

    def remote(src, dst, send, recv, target):
        return pltpu.make_async_remote_copy(
            src_ref=src, dst_ref=dst, send_sem=send, recv_sem=recv,
            device_id={"ep": target}, device_id_type=pl.DeviceIdType.MESH,
        )

    def gather(h, b, way):
        target = {UP: me + 4, DOWN: me - 4, ACROSS: across, MATE: mate}[way]
        part = rows_all.at[rows(b), spans[h]]
        return remote(part, part, ag_send.at[h, way, b], ag_recv.at[h, b], target)

    def send(cond, h, b, way):
        @pl.when(cond)
        def _():
            gather(h, b, way).start()

        pending.append((cond, lambda: gather(h, b, way).wait_send()))

    def arrived(h, b):
        gather(h, b, MATE).wait_recv()

    gates = gates_ref[...]
    share = gates / jnp.sum(gates, axis=1, keepdims=True)
    picks = routing_ref[...]
    lane = lax.broadcasted_iota(jnp.int32, (count, EXTRA), 1)
    expert = jnp.where(lane < experts, lane, lane - experts)
    spread = jnp.zeros((count, EXTRA), jnp.float32)
    for k in range(picks.shape[1]):
        spread = spread + jnp.where(picks[:, k : k + 1] == expert, share[:, k : k + 1], 0.0)
    high = spread.astype(jnp.bfloat16).astype(jnp.float32)
    extra = jnp.where(lane < experts, high, spread - high)
    rows_all[rows(me), pl.ds(0, width)] = x_ref[...]
    rows_all[rows(me), pl.ds(width, EXTRA)] = extra.astype(jnp.bfloat16)

    barrier = pltpu.get_barrier_semaphore()

    def hello(target):
        pl.semaphore_signal(
            barrier, inc=1, device_id={"ep": target}, device_id_type=pl.DeviceIdType.MESH
        )

    hello(mate)
    hello(across)
    pl.when(has_up)(lambda: hello(me + 4))
    pl.when(has_down)(lambda: hello(me - 4))
    pl.semaphore_wait(barrier, jnp.where(edge, 3, 4))

    for h in (1, 0):
        send(everyone, h, me, ACROSS)
        send(has_up, h, me, UP)
        send(has_down, h, me, DOWN)
        send(everyone, h, me, MATE)
    arrived(1, across)
    send(has_up, 1, across, UP)
    send(has_down, 1, across, DOWN)
    send(everyone, 1, across, MATE)

    def forward(distance):
        for step, onward, way in ((-distance, has_up, UP), (distance, has_down, DOWN)):
            other = layer + step
            present = other >= 0 if step < 0 else other <= last
            both = jnp.logical_and(present, onward)
            for h, s in ((1, side), (1, 1 - side), (0, side)):
                b = block(other, s, core)
                pl.when(present)(lambda h=h, b=b: arrived(h, b))
                send(both, h, b, way)
                if h == 0:
                    send(present, h, b, ACROSS)
                send(present, h, b, MATE)

    def order(step):
        first = (0, 1, 2, 3)[step]
        second = (1, 0, 2, 3)[step]
        near = jnp.where(edge, first, second)
        return jnp.where(layer < 2, near, last - near)

    def mlp(now):
        where = pl.ds(pl.multiple_of(now * 4 * count, 4 * count), 4 * count)
        wide = 256

        @pl.loop(0, hid // wide)
        def _(j):
            at = pl.multiple_of(j * wide, wide)
            x = rows_all[where, pl.ds(0, width)]
            gate = jnp.dot(x, w_up[:, pl.ds(at, wide)], preferred_element_type=jnp.float32)
            up = jnp.dot(
                x, w_up[:, pl.ds(pl.multiple_of(hid + at, wide), wide)],
                preferred_element_type=jnp.float32,
            )
            hidden[:, pl.ds(at, wide)] = (jax.nn.silu(gate) * up).astype(jnp.bfloat16)

        shares = rows_all[where, pl.ds(width, EXTRA)].astype(jnp.float32)
        lanes = lax.broadcasted_iota(jnp.int32, shares.shape, 1)
        mine = jnp.logical_or(lanes == me, lanes == me + experts)
        weight = jnp.sum(jnp.where(mine, shares, 0.0), axis=1, keepdims=True)

        @pl.loop(0, width // wide)
        def _(j):
            at = pl.ds(pl.multiple_of(j * wide, wide), wide)
            answer = jnp.dot(hidden[...], w_down[:, at], preferred_element_type=jnp.float32)
            answer = answer.astype(jnp.bfloat16).astype(jnp.float32)
            sums[where, at] = (weight * answer).astype(jnp.bfloat16)

    def piece(p):
        return pl.ds(pl.multiple_of(p * PIECE, PIECE), PIECE)

    pieces = width // PIECE

    def to_mate(now, s):
        slot = now * 2 + s
        return remote(
            sums.at[rows(block(now, s, 1 - core))], from_mate.at[rows(slot)],
            mate_send.at[slot], mate_recv.at[slot], mate,
        )

    def to_across(now, p):
        return remote(
            sums.at[rows(block(now, 1 - side, core)), piece(p)], from_across.at[rows(now), piece(p)],
            across_send.at[now, p], across_recv.at[now, p], across,
        )

    def to_layer(now, p):
        upward = now > layer
        slot = jnp.where(jnp.logical_and(now < layer, now == layer - 1), LAYERS, now)
        return remote(
            sums.at[rows(block(now, side, core)), piece(p)], from_layer.at[rows(slot), piece(p)],
            chain_send.at[now, p], chain_recv.at[slot, p], jnp.where(upward, me + 4, me - 4),
        )

    def chain_arrived(slot, p):
        part = from_layer.at[rows(slot), piece(p)]
        remote(part, part, chain_send.at[0, p], chain_recv.at[slot, p], mate).wait_recv()

    def wide32(ref, *index):
        return ref[index].astype(jnp.float32)

    def pair(now):
        to_mate(now, 1 - side).wait_recv()

        @pl.loop(0, pieces)
        def _(p):
            b, slot = block(now, 1 - side, core), now * 2 + 1 - side
            value = wide32(sums, rows(b), piece(p)) + wide32(from_mate, rows(slot), piece(p))
            sums[rows(b), piece(p)] = value.astype(jnp.bfloat16)
            to_across(now, p).start()

        to_mate(now, side).wait_recv()

    def held(now, p):
        to_across(now, p).wait_recv()
        b, slot = block(now, side, core), now * 2 + side
        value = wide32(sums, rows(b), piece(p)) + wide32(from_mate, rows(slot), piece(p))
        return value + wide32(from_across, rows(now), piece(p))

    def chain(now, incoming):
        @pl.loop(0, pieces)
        def _(p):
            value = held(now, p)
            if incoming:
                chain_arrived(now, p)
                value = value + wide32(from_layer, rows(now), piece(p))
            sums[rows(block(now, side, core)), piece(p)] = value.astype(jnp.bfloat16)
            to_layer(now, p).start()

    for step in range(LAYERS):
        now = order(step)
        if step > 0:
            forward(step)
        arrived(0, block(now, 1 - side, core))
        send(everyone, 0, block(now, 1 - side, core), MATE)
        for s in range(2):
            for h in range(2):
                arrived(h, block(now, s, 1 - core))
        if step == 0:
            up_copy.wait()
            down_copy.wait()
        mlp(now)
        to_mate(now, 1 - side).start()
        to_mate(now, side).start()
        pair(now)
        if step > 1:
            pl.when(edge)(lambda step=step: chain(order(step - 1), False))

    @pl.when(edge)
    def _():
        chain(order(3), False)

    @pl.when(jnp.logical_not(edge))
    def _():
        for step in (2, 3, 1):
            chain(order(step), True)

    @pl.loop(0, pieces)
    def _(p):
        value = held(layer, p)
        pl.when(has_down)(lambda: chain_arrived(layer, p))
        pl.when(has_up)(lambda: chain_arrived(LAYERS, p))
        below = wide32(from_layer, rows(layer), piece(p))
        above = wide32(from_layer, rows(LAYERS), piece(p))
        value = value + jnp.where(has_down, below, 0.0) + jnp.where(has_up, above, 0.0)
        out_ref[:, piece(p)] = value.astype(jnp.bfloat16)

    for cond, wait in pending:
        pl.when(cond)(wait)
    for step in range(LAYERS):
        now = order(step)
        to_mate(now, 0).wait_send()
        to_mate(now, 1).wait_send()

        @pl.loop(0, pieces)
        def _(p):
            to_across(now, p).wait_send()
            if step > 0:
                to_layer(now, p).wait_send()


def grid_experts(expert_input, routing, gate_weights, w_gate_up, w_down):
    count, width = expert_input.shape
    devices = LAYERS * 4
    pieces = width // PIECE
    dma = pltpu.SemaphoreType.DMA
    vmem, anywhere = pl.BlockSpec(memory_space=pltpu.VMEM), pl.BlockSpec(memory_space=pl.ANY)
    return pl.pallas_call(
        expert_kernel,
        out_shape=jax.ShapeDtypeStruct((count, width), jnp.bfloat16),
        in_specs=[vmem, vmem, vmem, anywhere, anywhere],
        out_specs=vmem,
        scratch_shapes=[
            pltpu.VMEM((devices * count, width + EXTRA), jnp.bfloat16),
            pltpu.VMEM((devices * count, width), jnp.bfloat16),
            pltpu.VMEM((LAYERS * 2 * count, width), jnp.bfloat16),
            pltpu.VMEM((LAYERS * count, width), jnp.bfloat16),
            pltpu.VMEM(((LAYERS + 1) * count, width), jnp.bfloat16),
            pltpu.VMEM(w_gate_up.shape, jnp.bfloat16),
            pltpu.VMEM(w_down.shape, jnp.bfloat16),
            pltpu.VMEM((4 * count, w_down.shape[0]), jnp.bfloat16),
            dma((2,)),
            dma((2, 4, devices)),
            dma((2, devices)),
            dma((LAYERS * 2,)),
            dma((LAYERS * 2,)),
            dma((LAYERS, pieces)),
            dma((LAYERS, pieces)),
            dma((LAYERS, pieces)),
            dma((LAYERS + 1, pieces)),
        ],
        compiler_params=pltpu.CompilerParams(
            collective_id=0, has_side_effects=True, vmem_limit_bytes=44 * 1024 * 1024
        ),
        name="expert_grid",
    )(expert_input, routing, gate_weights, w_gate_up, w_down)


def local(
    query,
    fresh_key,
    fresh_value,
    stored_keys,
    stored_values,
    lengths,
    q_gain,
    key_norm_gain,
    expert_input,
    routing,
    gate_weights,
    w_gate_up,
    w_down,
):
    attention_out = attention(
        query, fresh_key, fresh_value, stored_keys, stored_values, lengths, q_gain, key_norm_gain
    )
    devices = lax.axis_size("ep")
    if devices == LAYERS * 4:
        expert_out = grid_experts(expert_input, routing, gate_weights, w_gate_up[0], w_down[0])
        return (attention_out, expert_out)
    experts_all = devices * w_gate_up.shape[0]
    rows, width = expert_input.shape
    picks = routing.shape[1]
    capacity = 2 * rows * picks // experts_all
    share = gate_weights / jnp.sum(gate_weights, axis=1, keepdims=True)
    flat_ids = routing.reshape(-1)
    onehot = (flat_ids[:, None] == jnp.arange(experts_all)[None, :]).astype(jnp.int32)
    earlier = jnp.sum((jnp.cumsum(onehot, axis=0) - onehot) * onehot, axis=1)
    slot = flat_ids * capacity + earlier
    padded = jnp.concatenate([expert_input, jnp.zeros((1, width), jnp.bfloat16)], axis=0)
    sources = jnp.arange(rows * picks) // picks
    table = jnp.full((experts_all * capacity,), rows, jnp.int32).at[slot].set(sources)
    outgoing = padded[table].reshape(experts_all, capacity, width)
    arrived = lax.all_to_all(outgoing, "ep", split_axis=0, concat_axis=0, tiled=True)
    results = feed_forward(arrived, w_gate_up, w_down)
    returned = lax.all_to_all(results, "ep", split_axis=0, concat_axis=0, tiled=True)
    picked = returned.reshape(experts_all * capacity, width)[slot].reshape(rows, picks, width)
    mixed_output = jnp.zeros((rows, width), jnp.float32)
    for column in range(picks):
        mixed_output = mixed_output + share[:, column : column + 1] * picked[:, column].astype(
            jnp.float32
        )
    return (attention_out, mixed_output.astype(jnp.bfloat16))


def solution(mesh):
    return jax.shard_map(
        local,
        mesh=mesh,
        in_specs=(
            P(("group", "ep"), None),
            P(("group", "ep"), None),
            P(("group", "ep"), None),
            P(("group", "ep"), None, None),
            P(("group", "ep"), None, None),
            P(("group", "ep")),
            P(),
            P(),
            P(("group", "ep"), None),
            P(("group", "ep"), None),
            P(("group", "ep"), None),
            P("ep", None, None),
            P("ep", None, None),
        ),
        out_specs=(P(("group", "ep"), None), P(("group", "ep"), None)),
        check_vma=False,
    )
```

```python
import jax
import jax.numpy as jnp
from jax import lax
from jax.experimental import pallas as pl
from jax.experimental.pallas import tpu as pltpu
from jax.sharding import PartitionSpec as P

QUERY_HEADS = 32
KEY_VALUE_HEADS = 2
HEAD_SIZE = 128


def apply_rotation(all_values, positions):
    half = all_values.shape[-1] // 2
    steps = jnp.arange(half).astype(jnp.float32)
    inverse = jnp.exp(-2.0 * steps / all_values.shape[-1] * jnp.log(jnp.float32(1000000.0)))
    angles = positions.astype(jnp.float32)[:, None] * inverse[None, :]
    cosine = jnp.cos(angles)[:, None, :]
    sine = jnp.sin(angles)[:, None, :]
    first = all_values[..., :half]
    second = all_values[..., half:]
    return jnp.concatenate(
        [first * cosine - second * sine, second * cosine + first * sine], axis=-1
    )


def per_head_norm(all_values, gain):
    scale = lax.rsqrt(jnp.mean(all_values * all_values, axis=-1, keepdims=True) + 1e-06)
    return all_values * scale * gain


def attention(
    query, fresh_key, fresh_value, stored_keys, stored_values, lengths, q_gain, key_norm_gain
):
    token_count = query.shape[0]
    context_output = stored_keys.shape[1]
    query_groups = QUERY_HEADS // KEY_VALUE_HEADS
    normalized_query = apply_rotation(
        per_head_norm(
            query.astype(jnp.float32).reshape(token_count, QUERY_HEADS, HEAD_SIZE), q_gain
        ),
        lengths,
    ).astype(jnp.bfloat16)
    normalized_key = apply_rotation(
        per_head_norm(
            fresh_key.astype(jnp.float32).reshape(token_count, KEY_VALUE_HEADS, HEAD_SIZE),
            key_norm_gain,
        ),
        lengths,
    ).astype(jnp.bfloat16)
    grouped_queries = normalized_query.reshape(
        token_count, KEY_VALUE_HEADS, query_groups, HEAD_SIZE
    )
    all_keys = stored_keys.reshape(token_count, context_output, KEY_VALUE_HEADS, HEAD_SIZE)
    scores = jnp.einsum(
        "rhgd,rchd->rhgc", grouped_queries, all_keys, preferred_element_type=jnp.float32
    ) / jnp.sqrt(jnp.float32(HEAD_SIZE))
    own = jnp.sum(
        grouped_queries.astype(jnp.float32) * normalized_key.astype(jnp.float32)[:, :, None, :],
        axis=-1,
    ) / jnp.sqrt(jnp.float32(HEAD_SIZE))
    live = jnp.arange(context_output)[None, :] < lengths[:, None]
    scores = jnp.where(live[:, None, None, :], scores, -jnp.inf)
    top = jnp.maximum(jnp.max(scores, axis=-1), own)
    weights = jnp.exp(scores - top[..., None])
    own_weight = jnp.exp(own - top)
    total = jnp.sum(weights, axis=-1) + own_weight
    probs = (weights / total[..., None]).astype(jnp.bfloat16)
    fresh_token_prob = (own_weight / total).astype(jnp.bfloat16)
    all_values = stored_values.reshape(token_count, context_output, KEY_VALUE_HEADS, HEAD_SIZE)
    mixed_output = jnp.einsum(
        "rhgc,rchd->rhgd", probs, all_values, preferred_element_type=jnp.float32
    )
    mixed_output = mixed_output + fresh_token_prob.astype(jnp.float32)[
        ..., None
    ] * fresh_value.astype(jnp.float32).reshape(token_count, KEY_VALUE_HEADS, 1, HEAD_SIZE)
    return mixed_output.reshape(token_count, QUERY_HEADS * HEAD_SIZE).astype(jnp.bfloat16)


def feed_forward(slots, w_gate_up, w_down):
    layout = slots.shape
    flat = slots.reshape(-1, layout[-1])
    hidden_units = w_down.shape[1]
    both = jnp.dot(flat, w_gate_up[0], preferred_element_type=jnp.float32)
    hidden = (jax.nn.silu(both[:, :hidden_units]) * both[:, hidden_units:]).astype(jnp.bfloat16)
    answer = jnp.dot(hidden, w_down[0], preferred_element_type=jnp.float32).astype(jnp.bfloat16)
    return answer.reshape(layout)


LAYERS = 4
EXTRA = 128
Y_FIRST = 768
PIECE = 512
UP, DOWN, ACROSS, MATE = 0, 1, 2, 3


def attend(
    q_ref, key_ref, value_ref, lengths_ref, q_gain_ref, key_gain_ref, keys, values, queries_at,
    mixed_at, out_ref,
):
    half = HEAD_SIZE // 2
    queries = q_ref.shape[1] // HEAD_SIZE
    queries_each = queries // KEY_VALUE_HEADS
    lane = lax.broadcasted_iota(jnp.int32, (1, HEAD_SIZE), 1)
    steps = jnp.where(lane < half, lane, lane - half).astype(jnp.float32)
    inverse = jnp.exp(-2.0 * steps / HEAD_SIZE * jnp.log(jnp.full(steps.shape, 1000000.0)))
    token = lax.broadcasted_iota(jnp.int32, (keys.shape[0], 1), 0)
    lengths = jnp.zeros(token.shape, jnp.int32)
    for r in range(keys.shape[0]):
        lengths = jnp.where(token == r, lengths_ref[r], lengths)
    angles = lengths.astype(jnp.float32) * inverse
    cosine = jnp.cos(angles)
    sine = jnp.where(lane < half, -jnp.sin(angles), jnp.sin(angles))
    fresh_keys = key_ref[...].astype(jnp.float32)
    fresh_values = value_ref[...].astype(jnp.float32)
    root = jnp.sqrt(jnp.full((1, 1), float(HEAD_SIZE)))

    def turned(v, gain):
        scale = lax.rsqrt(jnp.mean(v * v, axis=-1, keepdims=True) + 1e-06)
        v = v * scale * gain
        swapped = jnp.concatenate([v[:, half:], v[:, :half]], axis=-1)
        return (v * cosine + swapped * sine).astype(jnp.bfloat16).astype(jnp.float32)

    for h in range(queries):
        at = slice(h * HEAD_SIZE, (h + 1) * HEAD_SIZE)
        v = turned(q_ref[:, at].astype(jnp.float32), q_gain_ref[...])
        for r in range(keys.shape[0]):
            queries_at[r * queries + h : r * queries + h + 1, :] = v[r : r + 1]
    fresh_turned = [
        turned(fresh_keys[:, h * HEAD_SIZE : (h + 1) * HEAD_SIZE], key_gain_ref[...])
        for h in range(KEY_VALUE_HEADS)
    ]

    for r in range(keys.shape[0]):
        for h in range(KEY_VALUE_HEADS):
            columns = slice(h * HEAD_SIZE, (h + 1) * HEAD_SIZE)
            start = r * queries + h * queries_each
            mine = queries_at[start : start + queries_each, :].astype(jnp.bfloat16)
            scores = lax.dot_general(
                mine, keys[r, :, columns], (((1,), (1,)), ((), ())),
                preferred_element_type=jnp.float32,
            ) / root
            own = jnp.sum(mine.astype(jnp.float32) * fresh_turned[h][r : r + 1], axis=-1, keepdims=True) / root
            position = lax.broadcasted_iota(jnp.int32, scores.shape, 1)
            scores = jnp.where(position < lengths_ref[r], scores, -jnp.inf)
            top = jnp.maximum(jnp.max(scores, axis=-1, keepdims=True), own)
            weights = jnp.exp(scores - top)
            own_weight = jnp.exp(own - top)
            total = jnp.sum(weights, axis=-1, keepdims=True) + own_weight
            probs = (weights / total).astype(jnp.bfloat16)
            own_prob = (own_weight / total).astype(jnp.bfloat16).astype(jnp.float32)
            mixed = jnp.dot(probs, values[r, :, columns], preferred_element_type=jnp.float32)
            mixed = mixed + own_prob * fresh_values[r : r + 1, columns]
            for g in range(queries_each):
                at = (h * queries_each + g) * HEAD_SIZE
                mixed_at[r : r + 1, at : at + HEAD_SIZE] = mixed[g : g + 1]
    out_ref[...] = mixed_at[...].astype(jnp.bfloat16)


def expert_kernel(
    x_ref, routing_ref, gates_ref, q_ref, key_ref, value_ref, lengths_ref, q_gain_ref, key_gain_ref,
    keys_hbm, values_hbm, up_hbm, down_hbm, out_ref, attended_ref, keys, values, queries_at,
    mixed_at,
    rows_all, sums, from_mate, from_across, from_layer, w_up, w_down, hidden,
    w_sem, ag_send, ag_recv, mate_send, mate_recv, across_send, across_recv, chain_send, chain_recv,
):
    me = lax.axis_index("ep")
    core, side, layer = lax.rem(me, 2), lax.rem(me // 2, 2), me // 4
    last = LAYERS - 1
    experts = LAYERS * 4
    count, width = x_ref.shape
    total = width + EXTRA
    hid = w_down.shape[0]
    mate, across = me + 1 - 2 * core, me + 2 - 4 * side
    has_up, has_down = layer < last, layer > 0
    edge = jnp.logical_or(layer == 0, layer == last)
    everyone = layer >= 0
    spans = (pl.ds(Y_FIRST, total - Y_FIRST), pl.ds(0, Y_FIRST))
    pending = []

    up_copy = pltpu.make_async_copy(up_hbm, w_up, w_sem.at[0])
    down_copy = pltpu.make_async_copy(down_hbm, w_down, w_sem.at[1])
    keys_copy = pltpu.make_async_copy(keys_hbm, keys, w_sem.at[2])
    values_copy = pltpu.make_async_copy(values_hbm, values, w_sem.at[3])
    keys_copy.start()
    values_copy.start()
    up_copy.start()
    down_copy.start()

    def block(l, s, c):
        return (l * 2 + s) * 2 + c

    def rows(b):
        return pl.ds(pl.multiple_of(b * count, count), count)

    def remote(src, dst, send, recv, target):
        return pltpu.make_async_remote_copy(
            src_ref=src, dst_ref=dst, send_sem=send, recv_sem=recv,
            device_id={"ep": target}, device_id_type=pl.DeviceIdType.MESH,
        )

    def gather(h, b, way):
        target = {UP: me + 4, DOWN: me - 4, ACROSS: across, MATE: mate}[way]
        part = rows_all.at[rows(b), spans[h]]
        return remote(part, part, ag_send.at[h, way, b], ag_recv.at[h, b], target)

    def send(cond, h, b, way):
        @pl.when(cond)
        def _():
            gather(h, b, way).start()

        pending.append((cond, lambda: gather(h, b, way).wait_send()))

    def arrived(h, b):
        gather(h, b, MATE).wait_recv()

    gates = gates_ref[...]
    share = gates / jnp.sum(gates, axis=0, keepdims=True)
    picks = routing_ref[...]
    place = lax.broadcasted_iota(jnp.int32, (EXTRA, count), 0)
    expert = jnp.where(place < experts, place, place - experts)
    spread = jnp.zeros((EXTRA, count), jnp.float32)
    for k in range(picks.shape[0]):
        spread = spread + jnp.where(picks[k : k + 1, :] == expert, share[k : k + 1, :], 0.0)
    high = spread.astype(jnp.bfloat16).astype(jnp.float32)
    extra = jnp.where(place < experts, high, spread - high).T
    rows_all[rows(me), pl.ds(0, width)] = x_ref[...]
    rows_all[rows(me), pl.ds(width, EXTRA)] = extra.astype(jnp.bfloat16)

    barrier = pltpu.get_barrier_semaphore()

    def hello(target):
        pl.semaphore_signal(
            barrier, inc=1, device_id={"ep": target}, device_id_type=pl.DeviceIdType.MESH
        )

    hello(mate)
    hello(across)
    pl.when(has_up)(lambda: hello(me + 4))
    pl.when(has_down)(lambda: hello(me - 4))
    pl.semaphore_wait(barrier, jnp.where(edge, 3, 4))

    for h in (1, 0):
        send(everyone, h, me, ACROSS)
        send(has_up, h, me, UP)
        send(has_down, h, me, DOWN)
        send(everyone, h, me, MATE)
    arrived(1, across)
    send(has_up, 1, across, UP)
    send(has_down, 1, across, DOWN)
    send(everyone, 1, across, MATE)

    keys_copy.wait()
    values_copy.wait()
    attend(
        q_ref, key_ref, value_ref, lengths_ref, q_gain_ref, key_gain_ref, keys, values, queries_at,
        mixed_at, attended_ref,
    )

    def forward(distance):
        for step, onward, way in ((-distance, has_up, UP), (distance, has_down, DOWN)):
            other = layer + step
            present = other >= 0 if step < 0 else other <= last
            both = jnp.logical_and(present, onward)
            for h, s in ((1, side), (1, 1 - side), (0, side)):
                b = block(other, s, core)
                pl.when(present)(lambda h=h, b=b: arrived(h, b))
                send(both, h, b, way)
                if h == 0:
                    send(present, h, b, ACROSS)
                send(present, h, b, MATE)

    def order(step):
        first = (0, 1, 2, 3)[step]
        second = (1, 0, 2, 3)[step]
        near = jnp.where(edge, first, second)
        return jnp.where(layer < 2, near, last - near)

    def mlp(now):
        where = pl.ds(pl.multiple_of(now * 4 * count, 4 * count), 4 * count)
        wide = 256

        @pl.loop(0, hid // wide)
        def _(j):
            at = pl.multiple_of(j * wide, wide)
            x = rows_all[where, pl.ds(0, width)]
            gate = jnp.dot(x, w_up[:, pl.ds(at, wide)], preferred_element_type=jnp.float32)
            up = jnp.dot(
                x, w_up[:, pl.ds(pl.multiple_of(hid + at, wide), wide)],
                preferred_element_type=jnp.float32,
            )
            hidden[:, pl.ds(at, wide)] = (jax.nn.silu(gate) * up).astype(jnp.bfloat16)

        shares = rows_all[where, pl.ds(width, EXTRA)].astype(jnp.float32)
        lanes = lax.broadcasted_iota(jnp.int32, shares.shape, 1)
        mine = jnp.logical_or(lanes == me, lanes == me + experts)
        weight = jnp.sum(jnp.where(mine, shares, 0.0), axis=1, keepdims=True)

        @pl.loop(0, width // wide)
        def _(j):
            at = pl.ds(pl.multiple_of(j * wide, wide), wide)
            answer = jnp.dot(hidden[...], w_down[:, at], preferred_element_type=jnp.float32)
            answer = answer.astype(jnp.bfloat16).astype(jnp.float32)
            sums[where, at] = (weight * answer).astype(jnp.bfloat16)

    def piece(p):
        return pl.ds(pl.multiple_of(p * PIECE, PIECE), PIECE)

    pieces = width // PIECE

    def to_mate(now, s):
        slot = now * 2 + s
        return remote(
            sums.at[rows(block(now, s, 1 - core))], from_mate.at[rows(slot)],
            mate_send.at[slot], mate_recv.at[slot], mate,
        )

    def to_across(now, p):
        return remote(
            sums.at[rows(block(now, 1 - side, core)), piece(p)], from_across.at[rows(now), piece(p)],
            across_send.at[now, p], across_recv.at[now, p], across,
        )

    def to_layer(now, p):
        upward = now > layer
        slot = jnp.where(jnp.logical_and(now < layer, now == layer - 1), LAYERS, now)
        return remote(
            sums.at[rows(block(now, side, core)), piece(p)], from_layer.at[rows(slot), piece(p)],
            chain_send.at[now, p], chain_recv.at[slot, p], jnp.where(upward, me + 4, me - 4),
        )

    def chain_arrived(slot, p):
        part = from_layer.at[rows(slot), piece(p)]
        remote(part, part, chain_send.at[0, p], chain_recv.at[slot, p], mate).wait_recv()

    def wide32(ref, *index):
        return ref[index].astype(jnp.float32)

    def pair(now):
        to_mate(now, 1 - side).wait_recv()

        @pl.loop(0, pieces)
        def _(p):
            b, slot = block(now, 1 - side, core), now * 2 + 1 - side
            value = wide32(sums, rows(b), piece(p)) + wide32(from_mate, rows(slot), piece(p))
            sums[rows(b), piece(p)] = value.astype(jnp.bfloat16)
            to_across(now, p).start()

        to_mate(now, side).wait_recv()

    def held(now, p):
        to_across(now, p).wait_recv()
        b, slot = block(now, side, core), now * 2 + side
        value = wide32(sums, rows(b), piece(p)) + wide32(from_mate, rows(slot), piece(p))
        return value + wide32(from_across, rows(now), piece(p))

    def chain(now, incoming):
        @pl.loop(0, pieces)
        def _(p):
            value = held(now, p)
            if incoming:
                chain_arrived(now, p)
                value = value + wide32(from_layer, rows(now), piece(p))
            sums[rows(block(now, side, core)), piece(p)] = value.astype(jnp.bfloat16)
            to_layer(now, p).start()

    for step in range(LAYERS):
        now = order(step)
        if step > 0:
            forward(step)
        arrived(0, block(now, 1 - side, core))
        send(everyone, 0, block(now, 1 - side, core), MATE)
        for s in range(2):
            for h in range(2):
                arrived(h, block(now, s, 1 - core))
        if step == 0:
            up_copy.wait()
            down_copy.wait()
        mlp(now)
        to_mate(now, 1 - side).start()
        to_mate(now, side).start()
        pair(now)
        if step > 1:
            pl.when(edge)(lambda step=step: chain(order(step - 1), False))

    @pl.when(edge)
    def _():
        chain(order(3), False)

    @pl.when(jnp.logical_not(edge))
    def _():
        for step in (2, 3, 1):
            chain(order(step), True)

    @pl.loop(0, pieces)
    def _(p):
        value = held(layer, p)
        pl.when(has_down)(lambda: chain_arrived(layer, p))
        pl.when(has_up)(lambda: chain_arrived(LAYERS, p))
        below = wide32(from_layer, rows(layer), piece(p))
        above = wide32(from_layer, rows(LAYERS), piece(p))
        value = value + jnp.where(has_down, below, 0.0) + jnp.where(has_up, above, 0.0)
        out_ref[:, piece(p)] = value.astype(jnp.bfloat16)

    for cond, wait in pending:
        pl.when(cond)(wait)
    for step in range(LAYERS):
        now = order(step)
        to_mate(now, 0).wait_send()
        to_mate(now, 1).wait_send()

        @pl.loop(0, pieces)
        def _(p):
            to_across(now, p).wait_send()
            if step > 0:
                to_layer(now, p).wait_send()


def grid_step(
    query, fresh_key, fresh_value, stored_keys, stored_values, lengths, q_gain, key_norm_gain,
    expert_input, routing, gate_weights, w_gate_up, w_down,
):
    count, width = expert_input.shape
    devices = LAYERS * 4
    pieces = width // PIECE
    dma = pltpu.SemaphoreType.DMA
    vmem, anywhere = pl.BlockSpec(memory_space=pltpu.VMEM), pl.BlockSpec(memory_space=pl.ANY)
    expert_out, attended = pl.pallas_call(
        expert_kernel,
        out_shape=(
            jax.ShapeDtypeStruct((count, width), jnp.bfloat16),
            jax.ShapeDtypeStruct(query.shape, jnp.bfloat16),
        ),
        in_specs=[vmem] * 6
        + [pl.BlockSpec(memory_space=pltpu.SMEM)]
        + [vmem] * 2
        + [anywhere] * 4,
        out_specs=(vmem, vmem),
        scratch_shapes=[
            pltpu.VMEM(stored_keys.shape, jnp.bfloat16),
            pltpu.VMEM(stored_values.shape, jnp.bfloat16),
            pltpu.VMEM((query.shape[0] * QUERY_HEADS, HEAD_SIZE), jnp.float32),
            pltpu.VMEM(query.shape, jnp.float32),
            pltpu.VMEM((devices * count, width + EXTRA), jnp.bfloat16),
            pltpu.VMEM((devices * count, width), jnp.bfloat16),
            pltpu.VMEM((LAYERS * 2 * count, width), jnp.bfloat16),
            pltpu.VMEM((LAYERS * count, width), jnp.bfloat16),
            pltpu.VMEM(((LAYERS + 1) * count, width), jnp.bfloat16),
            pltpu.VMEM(w_gate_up.shape, jnp.bfloat16),
            pltpu.VMEM(w_down.shape, jnp.bfloat16),
            pltpu.VMEM((4 * count, w_down.shape[0]), jnp.bfloat16),
            dma((4,)),
            dma((2, 4, devices)),
            dma((2, devices)),
            dma((LAYERS * 2,)),
            dma((LAYERS * 2,)),
            dma((LAYERS, pieces)),
            dma((LAYERS, pieces)),
            dma((LAYERS, pieces)),
            dma((LAYERS + 1, pieces)),
        ],
        compiler_params=pltpu.CompilerParams(
            collective_id=0, has_side_effects=True, vmem_limit_bytes=58 * 1024 * 1024
        ),
        name="expert_grid",
    )(
        expert_input, routing.T, gate_weights.T, query, fresh_key, fresh_value,
        lengths, q_gain[None, :], key_norm_gain[None, :],
        stored_keys, stored_values, w_gate_up, w_down,
    )
    return (attended, expert_out)


def local(
    query,
    fresh_key,
    fresh_value,
    stored_keys,
    stored_values,
    lengths,
    q_gain,
    key_norm_gain,
    expert_input,
    routing,
    gate_weights,
    w_gate_up,
    w_down,
):
    devices = lax.axis_size("ep")
    if devices == LAYERS * 4:
        return grid_step(
            query, fresh_key, fresh_value, stored_keys, stored_values, lengths, q_gain,
            key_norm_gain, expert_input, routing, gate_weights, w_gate_up[0], w_down[0],
        )
    attention_out = attention(
        query, fresh_key, fresh_value, stored_keys, stored_values, lengths, q_gain, key_norm_gain
    )
    experts_all = devices * w_gate_up.shape[0]
    rows, width = expert_input.shape
    picks = routing.shape[1]
    capacity = 2 * rows * picks // experts_all
    share = gate_weights / jnp.sum(gate_weights, axis=1, keepdims=True)
    flat_ids = routing.reshape(-1)
    onehot = (flat_ids[:, None] == jnp.arange(experts_all)[None, :]).astype(jnp.int32)
    earlier = jnp.sum((jnp.cumsum(onehot, axis=0) - onehot) * onehot, axis=1)
    slot = flat_ids * capacity + earlier
    padded = jnp.concatenate([expert_input, jnp.zeros((1, width), jnp.bfloat16)], axis=0)
    sources = jnp.arange(rows * picks) // picks
    table = jnp.full((experts_all * capacity,), rows, jnp.int32).at[slot].set(sources)
    outgoing = padded[table].reshape(experts_all, capacity, width)
    arrived = lax.all_to_all(outgoing, "ep", split_axis=0, concat_axis=0, tiled=True)
    results = feed_forward(arrived, w_gate_up, w_down)
    returned = lax.all_to_all(results, "ep", split_axis=0, concat_axis=0, tiled=True)
    picked = returned.reshape(experts_all * capacity, width)[slot].reshape(rows, picks, width)
    mixed_output = jnp.zeros((rows, width), jnp.float32)
    for column in range(picks):
        mixed_output = mixed_output + share[:, column : column + 1] * picked[:, column].astype(
            jnp.float32
        )
    return (attention_out, mixed_output.astype(jnp.bfloat16))


def solution(mesh):
    return jax.shard_map(
        local,
        mesh=mesh,
        in_specs=(
            P(("group", "ep"), None),
            P(("group", "ep"), None),
            P(("group", "ep"), None),
            P(("group", "ep"), None, None),
            P(("group", "ep"), None, None),
            P(("group", "ep")),
            P(),
            P(),
            P(("group", "ep"), None),
            P(("group", "ep"), None),
            P(("group", "ep"), None),
            P("ep", None, None),
            P("ep", None, None),
        ),
        out_specs=(P(("group", "ep"), None), P(("group", "ep"), None)),
        check_vma=False,
    )
```

```python
import jax
import jax.numpy as jnp
from jax import lax
from jax.experimental import pallas as pl
from jax.experimental.pallas import tpu as pltpu
from jax.sharding import PartitionSpec as P

QUERY_HEADS = 32
KEY_VALUE_HEADS = 2
HEAD_SIZE = 128


def apply_rotation(all_values, positions):
    half = all_values.shape[-1] // 2
    steps = jnp.arange(half).astype(jnp.float32)
    inverse = jnp.exp(-2.0 * steps / all_values.shape[-1] * jnp.log(jnp.float32(1000000.0)))
    angles = positions.astype(jnp.float32)[:, None] * inverse[None, :]
    cosine = jnp.cos(angles)[:, None, :]
    sine = jnp.sin(angles)[:, None, :]
    first = all_values[..., :half]
    second = all_values[..., half:]
    return jnp.concatenate(
        [first * cosine - second * sine, second * cosine + first * sine], axis=-1
    )


def per_head_norm(all_values, gain):
    scale = lax.rsqrt(jnp.mean(all_values * all_values, axis=-1, keepdims=True) + 1e-06)
    return all_values * scale * gain


def attention(
    query, fresh_key, fresh_value, stored_keys, stored_values, lengths, q_gain, key_norm_gain
):
    token_count = query.shape[0]
    context_output = stored_keys.shape[1]
    query_groups = QUERY_HEADS // KEY_VALUE_HEADS
    normalized_query = apply_rotation(
        per_head_norm(
            query.astype(jnp.float32).reshape(token_count, QUERY_HEADS, HEAD_SIZE), q_gain
        ),
        lengths,
    ).astype(jnp.bfloat16)
    normalized_key = apply_rotation(
        per_head_norm(
            fresh_key.astype(jnp.float32).reshape(token_count, KEY_VALUE_HEADS, HEAD_SIZE),
            key_norm_gain,
        ),
        lengths,
    ).astype(jnp.bfloat16)
    grouped_queries = normalized_query.reshape(
        token_count, KEY_VALUE_HEADS, query_groups, HEAD_SIZE
    )
    all_keys = stored_keys.reshape(token_count, context_output, KEY_VALUE_HEADS, HEAD_SIZE)
    scores = jnp.einsum(
        "rhgd,rchd->rhgc", grouped_queries, all_keys, preferred_element_type=jnp.float32
    ) / jnp.sqrt(jnp.float32(HEAD_SIZE))
    own = jnp.sum(
        grouped_queries.astype(jnp.float32) * normalized_key.astype(jnp.float32)[:, :, None, :],
        axis=-1,
    ) / jnp.sqrt(jnp.float32(HEAD_SIZE))
    live = jnp.arange(context_output)[None, :] < lengths[:, None]
    scores = jnp.where(live[:, None, None, :], scores, -jnp.inf)
    top = jnp.maximum(jnp.max(scores, axis=-1), own)
    weights = jnp.exp(scores - top[..., None])
    own_weight = jnp.exp(own - top)
    total = jnp.sum(weights, axis=-1) + own_weight
    probs = (weights / total[..., None]).astype(jnp.bfloat16)
    fresh_token_prob = (own_weight / total).astype(jnp.bfloat16)
    all_values = stored_values.reshape(token_count, context_output, KEY_VALUE_HEADS, HEAD_SIZE)
    mixed_output = jnp.einsum(
        "rhgc,rchd->rhgd", probs, all_values, preferred_element_type=jnp.float32
    )
    mixed_output = mixed_output + fresh_token_prob.astype(jnp.float32)[
        ..., None
    ] * fresh_value.astype(jnp.float32).reshape(token_count, KEY_VALUE_HEADS, 1, HEAD_SIZE)
    return mixed_output.reshape(token_count, QUERY_HEADS * HEAD_SIZE).astype(jnp.bfloat16)


def feed_forward(slots, w_gate_up, w_down):
    layout = slots.shape
    flat = slots.reshape(-1, layout[-1])
    hidden_units = w_down.shape[1]
    both = jnp.dot(flat, w_gate_up[0], preferred_element_type=jnp.float32)
    hidden = (jax.nn.silu(both[:, :hidden_units]) * both[:, hidden_units:]).astype(jnp.bfloat16)
    answer = jnp.dot(hidden, w_down[0], preferred_element_type=jnp.float32).astype(jnp.bfloat16)
    return answer.reshape(layout)


LAYERS = 4
EXTRA = 128
Y_FIRST = 768
PIECE = 512
UP, DOWN, ACROSS, MATE = 0, 1, 2, 3


def attend(
    q_ref, key_ref, value_ref, lengths_ref, q_gain_ref, key_gain_ref, keys, values, queries_at,
    mixed_at, out_ref,
):
    half = HEAD_SIZE // 2
    queries = q_ref.shape[1] // HEAD_SIZE
    queries_each = queries // KEY_VALUE_HEADS
    lane = lax.broadcasted_iota(jnp.int32, (1, HEAD_SIZE), 1)
    steps = jnp.where(lane < half, lane, lane - half).astype(jnp.float32)
    inverse = jnp.exp(-2.0 * steps / HEAD_SIZE * jnp.log(jnp.full(steps.shape, 1000000.0)))
    token = lax.broadcasted_iota(jnp.int32, (keys.shape[0], 1), 0)
    lengths = jnp.zeros(token.shape, jnp.int32)
    for r in range(keys.shape[0]):
        lengths = jnp.where(token == r, lengths_ref[r], lengths)
    angles = lengths.astype(jnp.float32) * inverse
    cosine = jnp.cos(angles)
    sine = jnp.where(lane < half, -jnp.sin(angles), jnp.sin(angles))
    fresh_keys = key_ref[...].astype(jnp.float32)
    fresh_values = value_ref[...].astype(jnp.float32)
    root = jnp.sqrt(jnp.full((1, 1), float(HEAD_SIZE)))

    def turned(v, gain):
        scale = lax.rsqrt(jnp.mean(v * v, axis=-1, keepdims=True) + 1e-06)
        v = v * scale * gain
        swapped = jnp.concatenate([v[:, half:], v[:, :half]], axis=-1)
        return (v * cosine + swapped * sine).astype(jnp.bfloat16).astype(jnp.float32)

    for h in range(queries):
        at = slice(h * HEAD_SIZE, (h + 1) * HEAD_SIZE)
        v = turned(q_ref[:, at].astype(jnp.float32), q_gain_ref[...])
        for r in range(keys.shape[0]):
            queries_at[r * queries + h : r * queries + h + 1, :] = v[r : r + 1]
    fresh_turned = [
        turned(fresh_keys[:, h * HEAD_SIZE : (h + 1) * HEAD_SIZE], key_gain_ref[...])
        for h in range(KEY_VALUE_HEADS)
    ]

    for r in range(keys.shape[0]):
        for h in range(KEY_VALUE_HEADS):
            columns = slice(h * HEAD_SIZE, (h + 1) * HEAD_SIZE)
            start = r * queries + h * queries_each
            mine = queries_at[start : start + queries_each, :].astype(jnp.bfloat16)
            scores = lax.dot_general(
                mine, keys[r, :, columns], (((1,), (1,)), ((), ())),
                preferred_element_type=jnp.float32,
            ) / root
            own = jnp.sum(mine.astype(jnp.float32) * fresh_turned[h][r : r + 1], axis=-1, keepdims=True) / root
            position = lax.broadcasted_iota(jnp.int32, scores.shape, 1)
            scores = jnp.where(position < lengths_ref[r], scores, -jnp.inf)
            top = jnp.maximum(jnp.max(scores, axis=-1, keepdims=True), own)
            weights = jnp.exp(scores - top)
            own_weight = jnp.exp(own - top)
            total = jnp.sum(weights, axis=-1, keepdims=True) + own_weight
            probs = (weights / total).astype(jnp.bfloat16)
            own_prob = (own_weight / total).astype(jnp.bfloat16).astype(jnp.float32)
            mixed = jnp.dot(probs, values[r, :, columns], preferred_element_type=jnp.float32)
            mixed = mixed + own_prob * fresh_values[r : r + 1, columns]
            for g in range(queries_each):
                at = (h * queries_each + g) * HEAD_SIZE
                mixed_at[r : r + 1, at : at + HEAD_SIZE] = mixed[g : g + 1]
    out_ref[...] = mixed_at[...].astype(jnp.bfloat16)


def expert_kernel(
    x_ref, routing_ref, gates_ref, q_ref, key_ref, value_ref, lengths_ref, q_gain_ref, key_gain_ref,
    keys_hbm, values_hbm, up_hbm, down_hbm, out_ref, attended_ref, keys, values, queries_at,
    mixed_at,
    rows_all, sums, from_mate, from_across, from_layer, w_up, w_down, hidden,
    w_sem, ag_send, ag_recv, mate_send, mate_recv, across_send, across_recv, chain_send, chain_recv,
):
    me = lax.axis_index("ep")
    core, side, layer = lax.rem(me, 2), lax.rem(me // 2, 2), me // 4
    last = LAYERS - 1
    experts = LAYERS * 4
    count, width = x_ref.shape
    total = width + EXTRA
    hid = w_down.shape[0]
    mate, across = me + 1 - 2 * core, me + 2 - 4 * side
    has_up, has_down = layer < last, layer > 0
    edge = jnp.logical_or(layer == 0, layer == last)
    everyone = layer >= 0
    spans = (pl.ds(Y_FIRST, total - Y_FIRST), pl.ds(0, Y_FIRST))
    pending = []

    up_copy = pltpu.make_async_copy(up_hbm, w_up, w_sem.at[0])
    down_copy = pltpu.make_async_copy(down_hbm, w_down, w_sem.at[1])
    keys_copy = pltpu.make_async_copy(keys_hbm, keys, w_sem.at[2])
    values_copy = pltpu.make_async_copy(values_hbm, values, w_sem.at[3])
    keys_copy.start()
    values_copy.start()
    up_copy.start()
    down_copy.start()

    def block(l, s, c):
        return (l * 2 + s) * 2 + c

    def rows(b):
        return pl.ds(pl.multiple_of(b * count, count), count)

    def remote(src, dst, send, recv, target):
        return pltpu.make_async_remote_copy(
            src_ref=src, dst_ref=dst, send_sem=send, recv_sem=recv,
            device_id={"ep": target}, device_id_type=pl.DeviceIdType.MESH,
        )

    def gather(h, b, way):
        target = {UP: me + 4, DOWN: me - 4, ACROSS: across, MATE: mate}[way]
        part = rows_all.at[rows(b), spans[h]]
        return remote(part, part, ag_send.at[h, way, b], ag_recv.at[h, b], target)

    def send(cond, h, b, way):
        @pl.when(cond)
        def _():
            gather(h, b, way).start()

        pending.append((cond, lambda: gather(h, b, way).wait_send()))

    def arrived(h, b):
        gather(h, b, MATE).wait_recv()

    gates = gates_ref[...]
    share = gates / jnp.sum(gates, axis=0, keepdims=True)
    picks = routing_ref[...]
    place = lax.broadcasted_iota(jnp.int32, (EXTRA, count), 0)
    expert = jnp.where(place < experts, place, place - experts)
    spread = jnp.zeros((EXTRA, count), jnp.float32)
    for k in range(picks.shape[0]):
        spread = spread + jnp.where(picks[k : k + 1, :] == expert, share[k : k + 1, :], 0.0)
    high = spread.astype(jnp.bfloat16).astype(jnp.float32)
    extra = jnp.where(place < experts, high, spread - high).T
    rows_all[rows(me), pl.ds(0, width)] = x_ref[...]
    rows_all[rows(me), pl.ds(width, EXTRA)] = extra.astype(jnp.bfloat16)

    barrier = pltpu.get_barrier_semaphore()

    def hello(target):
        pl.semaphore_signal(
            barrier, inc=1, device_id={"ep": target}, device_id_type=pl.DeviceIdType.MESH
        )

    hello(mate)
    hello(across)
    pl.when(has_up)(lambda: hello(me + 4))
    pl.when(has_down)(lambda: hello(me - 4))
    pl.semaphore_wait(barrier, jnp.where(edge, 3, 4))

    for h in (1, 0):
        send(everyone, h, me, ACROSS)
        send(has_up, h, me, UP)
        send(has_down, h, me, DOWN)
        send(everyone, h, me, MATE)
    arrived(1, across)
    send(has_up, 1, across, UP)
    send(has_down, 1, across, DOWN)
    send(everyone, 1, across, MATE)

    keys_copy.wait()
    values_copy.wait()
    attend(
        q_ref, key_ref, value_ref, lengths_ref, q_gain_ref, key_gain_ref, keys, values, queries_at,
        mixed_at, attended_ref,
    )

    def forward(distance):
        for step, onward, way in ((-distance, has_up, UP), (distance, has_down, DOWN)):
            other = layer + step
            present = other >= 0 if step < 0 else other <= last
            both = jnp.logical_and(present, onward)
            for h, s in ((1, side), (1, 1 - side), (0, side)):
                b = block(other, s, core)
                pl.when(present)(lambda h=h, b=b: arrived(h, b))
                send(both, h, b, way)
                if h == 0:
                    send(present, h, b, ACROSS)
                send(present, h, b, MATE)

    def order(step):
        first = (0, 1, 2, 3)[step]
        second = (1, 0, 2, 3)[step]
        near = jnp.where(edge, first, second)
        return jnp.where(layer < 2, near, last - near)

    def mlp(now):
        where = pl.ds(pl.multiple_of(now * 4 * count, 4 * count), 4 * count)
        wide = 256

        @pl.loop(0, hid // wide)
        def _(j):
            at = pl.multiple_of(j * wide, wide)
            x = rows_all[where, pl.ds(0, width)]
            gate = jnp.dot(x, w_up[:, pl.ds(at, wide)], preferred_element_type=jnp.float32)
            up = jnp.dot(
                x, w_up[:, pl.ds(pl.multiple_of(hid + at, wide), wide)],
                preferred_element_type=jnp.float32,
            )
            hidden[:, pl.ds(at, wide)] = (jax.nn.silu(gate) * up).astype(jnp.bfloat16)

        shares = rows_all[where, pl.ds(width, EXTRA)].astype(jnp.float32)
        lanes = lax.broadcasted_iota(jnp.int32, shares.shape, 1)
        mine = jnp.logical_or(lanes == me, lanes == me + experts)
        weight = jnp.sum(jnp.where(mine, shares, 0.0), axis=1, keepdims=True)

        @pl.loop(0, width // wide)
        def _(j):
            at = pl.ds(pl.multiple_of(j * wide, wide), wide)
            answer = jnp.dot(hidden[...], w_down[:, at], preferred_element_type=jnp.float32)
            answer = answer.astype(jnp.bfloat16).astype(jnp.float32)
            sums[where, at] = (weight * answer).astype(jnp.bfloat16)

    def piece(p):
        return pl.ds(pl.multiple_of(p * PIECE, PIECE), PIECE)

    pieces = width // PIECE

    def to_mate(now, s):
        slot = now * 2 + s
        return remote(
            sums.at[rows(block(now, s, 1 - core))], from_mate.at[rows(slot)],
            mate_send.at[slot], mate_recv.at[slot], mate,
        )

    def to_across(now, p):
        return remote(
            sums.at[rows(block(now, 1 - side, core)), piece(p)], from_across.at[rows(now), piece(p)],
            across_send.at[now, p], across_recv.at[now, p], across,
        )

    def to_layer(now, p):
        upward = now > layer
        slot = jnp.where(jnp.logical_and(now < layer, now == layer - 1), LAYERS, now)
        return remote(
            sums.at[rows(block(now, side, core)), piece(p)], from_layer.at[rows(slot), piece(p)],
            chain_send.at[now, p], chain_recv.at[slot, p], jnp.where(upward, me + 4, me - 4),
        )

    def chain_arrived(slot, p):
        part = from_layer.at[rows(slot), piece(p)]
        remote(part, part, chain_send.at[0, p], chain_recv.at[slot, p], mate).wait_recv()

    def wide32(ref, *index):
        return ref[index].astype(jnp.float32)

    def pair(now):
        to_mate(now, 1 - side).wait_recv()

        @pl.loop(0, pieces)
        def _(p):
            b, slot = block(now, 1 - side, core), now * 2 + 1 - side
            value = wide32(sums, rows(b), piece(p)) + wide32(from_mate, rows(slot), piece(p))
            sums[rows(b), piece(p)] = value.astype(jnp.bfloat16)
            to_across(now, p).start()

        to_mate(now, side).wait_recv()

    def held(now, p):
        to_across(now, p).wait_recv()
        b, slot = block(now, side, core), now * 2 + side
        value = wide32(sums, rows(b), piece(p)) + wide32(from_mate, rows(slot), piece(p))
        return value + wide32(from_across, rows(now), piece(p))

    def chain(now, incoming):
        @pl.loop(0, pieces)
        def _(p):
            value = held(now, p)
            if incoming:
                chain_arrived(now, p)
                value = value + wide32(from_layer, rows(now), piece(p))
            sums[rows(block(now, side, core)), piece(p)] = value.astype(jnp.bfloat16)
            to_layer(now, p).start()

    for step in range(LAYERS):
        now = order(step)
        arrived(0, block(now, 1 - side, core))
        send(everyone, 0, block(now, 1 - side, core), MATE)
        for s in range(2):
            for h in range(2):
                arrived(h, block(now, s, 1 - core))
        if step == 0:
            up_copy.wait()
            down_copy.wait()
        mlp(now)
        to_mate(now, 1 - side).start()
        to_mate(now, side).start()
        if step < LAYERS - 1:
            forward(step + 1)
        pair(now)
        if step > 1:
            pl.when(edge)(lambda step=step: chain(order(step - 1), False))

    @pl.when(edge)
    def _():
        chain(order(3), False)

    @pl.when(jnp.logical_not(edge))
    def _():
        for step in (2, 3, 1):
            chain(order(step), True)

    @pl.loop(0, pieces)
    def _(p):
        value = held(layer, p)
        pl.when(has_down)(lambda: chain_arrived(layer, p))
        pl.when(has_up)(lambda: chain_arrived(LAYERS, p))
        below = wide32(from_layer, rows(layer), piece(p))
        above = wide32(from_layer, rows(LAYERS), piece(p))
        value = value + jnp.where(has_down, below, 0.0) + jnp.where(has_up, above, 0.0)
        out_ref[:, piece(p)] = value.astype(jnp.bfloat16)

    for cond, wait in pending:
        pl.when(cond)(wait)
    for step in range(LAYERS):
        now = order(step)
        to_mate(now, 0).wait_send()
        to_mate(now, 1).wait_send()

        @pl.loop(0, pieces)
        def _(p):
            to_across(now, p).wait_send()
            if step > 0:
                to_layer(now, p).wait_send()


def grid_step(
    query, fresh_key, fresh_value, stored_keys, stored_values, lengths, q_gain, key_norm_gain,
    expert_input, routing, gate_weights, w_gate_up, w_down,
):
    count, width = expert_input.shape
    devices = LAYERS * 4
    pieces = width // PIECE
    dma = pltpu.SemaphoreType.DMA
    vmem, anywhere = pl.BlockSpec(memory_space=pltpu.VMEM), pl.BlockSpec(memory_space=pl.ANY)
    expert_out, attended = pl.pallas_call(
        expert_kernel,
        out_shape=(
            jax.ShapeDtypeStruct((count, width), jnp.bfloat16),
            jax.ShapeDtypeStruct(query.shape, jnp.bfloat16),
        ),
        in_specs=[vmem] * 6
        + [pl.BlockSpec(memory_space=pltpu.SMEM)]
        + [vmem] * 2
        + [anywhere] * 4,
        out_specs=(vmem, vmem),
        scratch_shapes=[
            pltpu.VMEM(stored_keys.shape, jnp.bfloat16),
            pltpu.VMEM(stored_values.shape, jnp.bfloat16),
            pltpu.VMEM((query.shape[0] * QUERY_HEADS, HEAD_SIZE), jnp.float32),
            pltpu.VMEM(query.shape, jnp.float32),
            pltpu.VMEM((devices * count, width + EXTRA), jnp.bfloat16),
            pltpu.VMEM((devices * count, width), jnp.bfloat16),
            pltpu.VMEM((LAYERS * 2 * count, width), jnp.bfloat16),
            pltpu.VMEM((LAYERS * count, width), jnp.bfloat16),
            pltpu.VMEM(((LAYERS + 1) * count, width), jnp.bfloat16),
            pltpu.VMEM(w_gate_up.shape, jnp.bfloat16),
            pltpu.VMEM(w_down.shape, jnp.bfloat16),
            pltpu.VMEM((4 * count, w_down.shape[0]), jnp.bfloat16),
            dma((4,)),
            dma((2, 4, devices)),
            dma((2, devices)),
            dma((LAYERS * 2,)),
            dma((LAYERS * 2,)),
            dma((LAYERS, pieces)),
            dma((LAYERS, pieces)),
            dma((LAYERS, pieces)),
            dma((LAYERS + 1, pieces)),
        ],
        compiler_params=pltpu.CompilerParams(
            collective_id=0, has_side_effects=True, vmem_limit_bytes=58 * 1024 * 1024
        ),
        name="expert_grid",
    )(
        expert_input, routing.T, gate_weights.T, query, fresh_key, fresh_value,
        lengths, q_gain[None, :], key_norm_gain[None, :],
        stored_keys, stored_values, w_gate_up, w_down,
    )
    return (attended, expert_out)


def local(
    query,
    fresh_key,
    fresh_value,
    stored_keys,
    stored_values,
    lengths,
    q_gain,
    key_norm_gain,
    expert_input,
    routing,
    gate_weights,
    w_gate_up,
    w_down,
):
    devices = lax.axis_size("ep")
    if devices == LAYERS * 4:
        return grid_step(
            query, fresh_key, fresh_value, stored_keys, stored_values, lengths, q_gain,
            key_norm_gain, expert_input, routing, gate_weights, w_gate_up[0], w_down[0],
        )
    attention_out = attention(
        query, fresh_key, fresh_value, stored_keys, stored_values, lengths, q_gain, key_norm_gain
    )
    experts_all = devices * w_gate_up.shape[0]
    rows, width = expert_input.shape
    picks = routing.shape[1]
    capacity = 2 * rows * picks // experts_all
    share = gate_weights / jnp.sum(gate_weights, axis=1, keepdims=True)
    flat_ids = routing.reshape(-1)
    onehot = (flat_ids[:, None] == jnp.arange(experts_all)[None, :]).astype(jnp.int32)
    earlier = jnp.sum((jnp.cumsum(onehot, axis=0) - onehot) * onehot, axis=1)
    slot = flat_ids * capacity + earlier
    padded = jnp.concatenate([expert_input, jnp.zeros((1, width), jnp.bfloat16)], axis=0)
    sources = jnp.arange(rows * picks) // picks
    table = jnp.full((experts_all * capacity,), rows, jnp.int32).at[slot].set(sources)
    outgoing = padded[table].reshape(experts_all, capacity, width)
    arrived = lax.all_to_all(outgoing, "ep", split_axis=0, concat_axis=0, tiled=True)
    results = feed_forward(arrived, w_gate_up, w_down)
    returned = lax.all_to_all(results, "ep", split_axis=0, concat_axis=0, tiled=True)
    picked = returned.reshape(experts_all * capacity, width)[slot].reshape(rows, picks, width)
    mixed_output = jnp.zeros((rows, width), jnp.float32)
    for column in range(picks):
        mixed_output = mixed_output + share[:, column : column + 1] * picked[:, column].astype(
            jnp.float32
        )
    return (attention_out, mixed_output.astype(jnp.bfloat16))


def solution(mesh):
    return jax.shard_map(
        local,
        mesh=mesh,
        in_specs=(
            P(("group", "ep"), None),
            P(("group", "ep"), None),
            P(("group", "ep"), None),
            P(("group", "ep"), None, None),
            P(("group", "ep"), None, None),
            P(("group", "ep")),
            P(),
            P(),
            P(("group", "ep"), None),
            P(("group", "ep"), None),
            P(("group", "ep"), None),
            P("ep", None, None),
            P("ep", None, None),
        ),
        out_specs=(P(("group", "ep"), None), P(("group", "ep"), None)),
        check_vma=False,
    )
```
